32 devices in a mesh: gx: 4 (over x, core), gy: 8 (over z, y).
Axes of the slice: x: 2, y: 2, z: 4, core: 2. Of those that a mesh axis runs over, the one named last changes fastest.
Arguments:
- values: float32 [8192, 128], P(('gx', 'gy')), may hold values from -6 to 6
- noise: float32 [8192, 128], P(('gx', 'gy')), may hold values from 0.1 to 1
- fractions: float32 [3, 8192, 128], P(None, ('gx', 'gy')), may hold values from 0 to 1
- cell_xy: int32 [2, 8192, 128], P(None, ('gx', 'gy')), may hold values from 0 to 7
- cell_z: int32 [8192, 128], P(('gx', 'gy')), may hold values from 0 to 255
- tile_grid: int32 [8192], P(('gx', 'gy')), may hold values from 0 to 127
- counts: int32 [8192], P(('gx', 'gy')), may hold values from 1 to 128, as said below
- rate_x: float32 [512], replicated, may hold values from 0.01 to 4
- rate_y: float32 [512], replicated, may hold values from 0.01 to 4
- rate_z: float32 [256], replicated, may hold values from 0.01 to 4
Outputs:
- product: float32 [8192, 128], P(('gx', 'gy'))
The draws below stay inside these ranges and needn't reach their ends.
Inputs may be any that keep to these rules, and one draw needn't show every extreme that they name: `counts`: every fifth point tile, counted from tile 0, is full. `tile_grid`: A point tile's grid tile is numbered within its own device's block of the grid.
All inputs are finite; a program needn't handle non-finite values.
Results may differ from the reference program's by a relative error of at most 0.00005.
Values sent between devices are 32-bit elements; how exact they have to be, the bound alone decides.
A program may use at most 128 MiB of HBM per device.

```python
import math
import jax
import jax.numpy as jnp
import numpy as np

NX = 512
NY = 512
NZ = 256
TILE = 8
PTS = 128
TILES_DEV = 256
TILES = 8192
GT_DEV = 128
N_GX = 4
N_GY = 8


def draw_counts(key, part):
    key = jax.random.fold_in(key, 7)
    drawn = jax.random.randint(key, (TILES,), 1, PTS + 1)
    slot_number = jnp.arange(TILES, dtype=jnp.int32)
    return jnp.where(slot_number % 5 == 0, PTS, drawn).astype(jnp.int32)


def touch_ends(result, rng, low, top_value):
    longest = result.shape.index(max(result.shape))
    spots = []
    for shift in (0, 1):
        where = [jax.random.randint(jax.random.fold_in(rng, axis), (), 0, length) for axis, length in enumerate(result.shape)]
        where[longest] = (where[longest] + shift) % result.shape[longest]
        spots.append(tuple(where))
    return result.at[spots[0]].set(low).at[spots[1]].set(top_value)


def shard_levels(rng, dims, cuts, least, high):
    def one(axis_at, parts):
        draws = jax.random.uniform(jax.random.fold_in(jax.random.fold_in(rng, 6), axis_at), (parts,), jnp.float32, least / len(cuts), high / len(cuts))
        return jnp.repeat(jnp.exp(draws), dims[axis_at] // parts).reshape((-1,) + (1,) * (len(dims) - axis_at - 1))

    factor_of = one(*cuts[0])
    for cut in cuts[1:]:
        factor_of = factor_of * one(*cut)
    return factor_of


def rank_bounds(number_of, lean):
    loads = [(1 << 20) // math.isqrt(rank ** lean) + 1 for rank in range(1, number_of + 1)]
    deviation = 1 + sum(loads) // (1 << 30)
    return np.cumsum(np.array([max(1, weight // deviation) for weight in loads]))


def ranked(rng, shape, number_of, lean):
    table = rank_bounds(number_of, lean)
    pick = jax.random.randint(jax.random.fold_in(rng, 1), shape, 0, int(table[number_of - 1]))
    standing = jnp.searchsorted(jnp.asarray(table, jnp.int32), pick, side="right")
    return jax.random.permutation(jax.random.fold_in(rng, 2), number_of)[standing].astype(jnp.int32)


def normal_values(key, shape, scale, limit, shards=(), kind=jnp.bfloat16):
    entries = scale * jax.random.normal(key, shape, jnp.float32)
    if shards:
        entries = entries * shard_levels(key, shape, shards, -0.22, 0.18)
    return jnp.clip(entries, -limit, limit).astype(kind)


def setup_inputs(seed: int = 0) -> dict:
    key_list = jax.random.split(jax.random.key(seed), 11)
    return {
        "values": normal_values(key_list[0], (TILES, PTS), 1.0, 6.0, ((0, 32),), jnp.float32),
        "noise": jnp.clip(jnp.exp(math.log(1.0) - 2.3025851 * jax.random.uniform(key_list[1], (TILES, PTS), jnp.float32) ** shard_levels(key_list[1], (TILES, PTS), ((0, 32),), -0.2, 0.2)), 0.1, 1.0),
        "fractions": jnp.clip(1.0 * jax.random.uniform(key_list[2], (3, TILES, PTS), jnp.float32) ** shard_levels(key_list[2], (3, TILES, PTS), ((1, 32),), -0.2, 0.2), 0.0, 1.0),
        "cell_xy": touch_ends(jax.random.randint(key_list[3], (2, TILES, PTS), 0, TILE), jax.random.fold_in(key_list[3], 1), 0, TILE - 1).astype(jnp.int32),
        "cell_z": touch_ends(jax.random.randint(key_list[4], (TILES, PTS), 0, NZ), jax.random.fold_in(key_list[4], 1), 0, NZ - 1).astype(jnp.int32),
        "tile_grid": touch_ends(ranked(key_list[5], (TILES,), GT_DEV, 2), jax.random.fold_in(key_list[5], 3), 0, GT_DEV - 1).astype(jnp.int32),
        "counts": draw_counts(jax.random.fold_in(key_list[10], 71), 0),
        "rate_x": jnp.clip(jnp.exp(jax.random.uniform(key_list[7], (NX,), jnp.float32, math.log(0.01), math.log(4.0))), 0.01, 4.0),
        "rate_y": jnp.clip(jnp.exp(jax.random.uniform(key_list[8], (NY,), jnp.float32, math.log(0.01), math.log(4.0))), 0.01, 4.0),
        "rate_z": jnp.clip(jnp.exp(jax.random.uniform(key_list[9], (NZ,), jnp.float32, math.log(0.01), math.log(4.0))), 0.01, 4.0),
    }


def cubic_taps(fraction):
    square = fraction * fraction
    cubed = square * fraction
    return (-0.5 * cubed + square - 0.5 * fraction,
            1.5 * cubed - 2.5 * square + 1.0,
            -1.5 * cubed + 2.0 * square + 0.5 * fraction,
            0.5 * cubed - 0.5 * square)


def hartley(grid_field, axis_number):
    spectrum = jnp.fft.fft(grid_field, axis=axis_number)
    return jnp.real(spectrum) - jnp.imag(spectrum)


def reference(values, noise, fractions, cell_xy, cell_z, tile_grid, counts, rate_x, rate_y, rate_z):
    cells_x = NX // N_GX
    cells_y = NY // N_GY
    rows_y = cells_y // TILE
    owner_dev = jnp.arange(TILES, dtype=jnp.int32) // TILES_DEV
    anchor_x = (owner_dev // N_GY) * cells_x + (tile_grid // rows_y) * TILE
    anchor_y = (owner_dev % N_GY) * cells_y + (tile_grid % rows_y) * TILE
    is_live = jnp.arange(PTS, dtype=jnp.int32)[None, :] < counts[:, None]
    source = jnp.where(is_live, values, 0.0)
    base_x = anchor_x[:, None] + cell_xy[0] - 1
    base_y = anchor_y[:, None] + cell_xy[1] - 1
    base_z = cell_z - 1
    taps_x = cubic_taps(fractions[0])
    taps_y = cubic_taps(fractions[1])
    taps_z = cubic_taps(fractions[2])
    spread = jnp.zeros((NX, NY, NZ), jnp.float32)
    for tap_x in range(4):
        index_x = (base_x + tap_x) % NX
        for tap_y in range(4):
            index_y = (base_y + tap_y) % NY
            weight_xy = taps_x[tap_x] * taps_y[tap_y]
            for tap_z in range(4):
                index_z = (base_z + tap_z) % NZ
                spread = spread.at[index_x, index_y, index_z].add(weight_xy * taps_z[tap_z] * source)
    coeffs = hartley(hartley(hartley(spread, 0), 1), 2)
    denom = 1.0 + rate_x[:, None, None] + rate_y[None, :, None] + rate_z[None, None, :]
    weighted = coeffs * (4.0 / (denom * denom))
    smooth = hartley(hartley(hartley(weighted, 0), 1), 2) / (NX * NY * NZ)
    sampled = jnp.zeros((TILES, PTS), jnp.float32)
    for tap_x in range(4):
        index_x = (base_x + tap_x) % NX
        for tap_y in range(4):
            index_y = (base_y + tap_y) % NY
            weight_xy = taps_x[tap_x] * taps_y[tap_y]
            for tap_z in range(4):
                index_z = (base_z + tap_z) % NZ
                sampled = sampled + weight_xy * taps_z[tap_z] * smooth[index_x, index_y, index_z]
    return jnp.where(is_live, noise * values + sampled, 0.0)
```

```python
import functools
import math

import jax
import jax.numpy as jnp
import numpy as np
from jax import lax
from jax.experimental import pallas as pl
from jax.experimental.pallas import tpu as pltpu
from jax.sharding import PartitionSpec as P

TILE = 8
SIDE = 11
WINDOW = 16
GROUP = 8
LOW = 1
HIGH = 2
VMEM_BYTES = 48 * 1024 * 1024


def ring(axis):
    count = lax.axis_size(axis)
    forward = [(i, (i + 1) % count) for i in range(count)]
    return forward, [(target, source) for source, target in forward]


def cubic_taps(fraction):
    square = fraction * fraction
    cubed = square * fraction
    return (
        -0.5 * cubed + square - 0.5 * fraction,
        1.5 * cubed - 2.5 * square + 1.0,
        -1.5 * cubed + 2.0 * square + 0.5 * fraction,
        0.5 * cubed - 0.5 * square,
    )


def cas_table(length):
    counter = np.arange(length, dtype=np.int64)
    radians = (counter[:, None] * counter[None, :] % length) * (2.0 * math.pi / length)
    return jnp.asarray((np.cos(radians) + np.sin(radians)).astype(np.float32))


def halves(array):
    top = array.astype(jnp.bfloat16)
    return top, (array - top.astype(jnp.float32)).astype(jnp.bfloat16)


def split_dot(left, right, dims):
    left_top, left_rest = halves(left)
    right_top, right_rest = halves(right)

    def dot(a, b):
        return lax.dot_general(a, b, (dims, ((), ())), preferred_element_type=jnp.float32)

    return dot(left_top, right_top) + (dot(left_top, right_rest) + dot(left_rest, right_top))


def box_weights(taps, start, row):
    delta = lax.broadcasted_iota(jnp.int32, (WINDOW, start.shape[1]), 0) - start[row : row + 1]
    weight = jnp.zeros(delta.shape, jnp.float32)
    for offset in range(4):
        weight = jnp.where(delta == offset, taps[offset][row : row + 1], weight)
    return weight


def column_weights(taps, start, row, depth):
    delta = lax.broadcasted_iota(jnp.int32, (depth, start.shape[1]), 0) - start[row : row + 1] + 1
    delta = jnp.where(delta < 0, delta + depth, delta)
    delta = jnp.where(delta >= depth, delta - depth, delta)
    weight = jnp.zeros(delta.shape, jnp.float32)
    for offset in range(4):
        weight = jnp.where(delta == offset, taps[offset][row : row + 1], weight)
    return weight


def group_rows(refs, first):
    return [ref[pl.ds(first, GROUP), :] for ref in refs]


def spread_kernel(
    rows_y, tile_grid, counts, values, fx, fy, fz, cx, cy, cz, padded
):
    depth = padded.shape[2]
    points = values.shape[1]
    padded[...] = jnp.zeros_like(padded)

    def step(index, carry):
        first = pl.multiple_of(index * GROUP, GROUP)
        value, f0, f1, f2, c0, c1, c2 = group_rows((values, fx, fy, fz, cx, cy, cz), first)
        taps_x, taps_y, taps_z = cubic_taps(f0), cubic_taps(f1), cubic_taps(f2)
        slot = lax.broadcasted_iota(jnp.int32, (1, points), 1)
        boxes = []
        for row in range(GROUP):
            source = jnp.where(slot < counts[first + row], value[row : row + 1], 0.0)
            wide_x = box_weights(taps_x, c0, row) * source
            wide_y = box_weights(taps_y, c1, row)
            plane = jnp.concatenate([wide_x[x : x + 1] * wide_y for x in range(SIDE)], 0)
            column = column_weights(taps_z, c2, row, depth)
            boxes.append(split_dot(plane, column, ((1,), (1,))))
        for row in range(GROUP):
            owner = tile_grid[first + row]
            at_x = (owner // rows_y) * TILE
            at_y = pl.multiple_of(lax.rem(owner, rows_y) * TILE, TILE)
            padded[pl.ds(at_x, SIDE), pl.ds(at_y, WINDOW), :] += boxes[row].reshape(
                SIDE, WINDOW, depth
            )
        return carry

    lax.fori_loop(0, values.shape[0] // GROUP, step, 0)


def sample_kernel(
    rows_y, tile_grid, counts, values, noise, fx, fy, fz, cx, cy, cz, field, product
):
    depth = field.shape[2]
    points = values.shape[1]

    def step(index, carry):
        first = pl.multiple_of(index * GROUP, GROUP)
        value, level, f0, f1, f2, c0, c1, c2 = group_rows(
            (values, noise, fx, fy, fz, cx, cy, cz), first
        )
        taps_x, taps_y, taps_z = cubic_taps(f0), cubic_taps(f1), cubic_taps(f2)
        slot = lax.broadcasted_iota(jnp.int32, (1, points), 1)
        rows = []
        for row in range(GROUP):
            owner = tile_grid[first + row]
            at_x = (owner // rows_y) * TILE
            at_y = pl.multiple_of(lax.rem(owner, rows_y) * TILE, TILE)
            box = field[pl.ds(at_x, SIDE), pl.ds(at_y, WINDOW), :].reshape(SIDE * WINDOW, depth)
            column = column_weights(taps_z, c2, row, depth)
            along = split_dot(box, column, ((1,), (0,))).reshape(SIDE, WINDOW, points)
            wide_x = box_weights(taps_x, c0, row)
            wide_y = box_weights(taps_y, c1, row)
            total = along[0] * wide_x[0:1]
            for x in range(1, SIDE):
                total = total + along[x] * wide_x[x : x + 1]
            sampled = jnp.sum(total * wide_y, axis=0, keepdims=True)
            result = level[row : row + 1] * value[row : row + 1] + sampled
            rows.append(jnp.where(slot < counts[first + row], result, 0.0))
        product[pl.ds(first, GROUP), :] = jnp.concatenate(rows, 0)
        return carry

    lax.fori_loop(0, values.shape[0] // GROUP, step, 0)


def body(values, noise, fractions, cell_xy, cell_z, tile_grid, counts, rate_x, rate_y, rate_z):
    tile_count, point_count = values.shape
    ranks_x = lax.axis_size("gx")
    ranks_y = lax.axis_size("gy")
    full_x = rate_x.shape[0]
    full_y = rate_y.shape[0]
    depth = rate_z.shape[0]
    cells_x = full_x // ranks_x
    cells_y = full_y // ranks_y
    rows_y = cells_y // TILE
    wide_x = cells_x + LOW + HIGH
    wide_y = cells_y + TILE
    smem = pl.BlockSpec(memory_space=pltpu.SMEM)
    vmem = pl.BlockSpec(memory_space=pltpu.VMEM)
    params = pltpu.CompilerParams(vmem_limit_bytes=VMEM_BYTES)
    places = (
        fractions[0], fractions[1], fractions[2], cell_xy[0], cell_xy[1], cell_z,
    )
    flops = 6 * tile_count * SIDE * WINDOW * point_count * depth
    cost = pl.CostEstimate(
        flops=flops, bytes_accessed=4 * wide_x * wide_y * depth, transcendentals=0
    )
    padded = pl.pallas_call(
        functools.partial(spread_kernel, rows_y),
        out_shape=jax.ShapeDtypeStruct((wide_x, wide_y, depth), jnp.float32),
        in_specs=[smem, smem] + [vmem] * 7,
        out_specs=vmem,
        compiler_params=params,
        cost_estimate=cost,
        name="spread",
    )(tile_grid, counts, values, *places)

    forward_x, backward_x = ring("gx")
    forward_y, backward_y = ring("gy")
    from_low = lax.ppermute(padded[cells_x + LOW :], "gx", forward_x)
    from_high = lax.ppermute(padded[:LOW], "gx", backward_x)
    padded = jnp.concatenate(
        [
            padded[LOW : LOW + HIGH] + from_low,
            padded[LOW + HIGH : cells_x],
            padded[cells_x : cells_x + LOW] + from_high,
        ],
        0,
    )
    from_low = lax.ppermute(
        padded[:, cells_y + LOW : cells_y + LOW + HIGH], "gy", forward_y
    )
    from_high = lax.ppermute(padded[:, :LOW], "gy", backward_y)
    spread_grid = jnp.concatenate(
        [
            padded[:, LOW : LOW + HIGH] + from_low,
            padded[:, LOW + HIGH : cells_y],
            padded[:, cells_y : cells_y + LOW] + from_high,
        ],
        1,
    )

    table_x = cas_table(full_x)
    table_y = cas_table(full_y)
    table_z = cas_table(depth)
    planes_dev = depth // (ranks_x * ranks_y)
    einsum = functools.partial(jnp.einsum, precision=lax.Precision.HIGH)
    turned = einsum("xyz,zk->xky", spread_grid, table_z)
    pencils = lax.all_to_all(turned, "gy", split_axis=1, concat_axis=2, tiled=True)
    pencils = einsum("xzy,yk->xzk", pencils, table_y)
    planes = lax.all_to_all(pencils, "gx", split_axis=1, concat_axis=0, tiled=True)
    z_start = lax.axis_index("gy") * (depth // ranks_y) + lax.axis_index("gx") * planes_dev
    planes = einsum("xzy,xk->kzy", planes, table_x)
    local_rate = lax.dynamic_slice_in_dim(rate_z, z_start, planes_dev)
    denom = 1.0 + rate_x[:, None, None] + rate_y[None, None, :] + local_rate[None, :, None]
    weighted = planes * ((4.0 / (full_x * full_y * depth)) / (denom * denom))
    inverse = einsum("kzy,kx->xzy", weighted, table_x)
    slabs = lax.all_to_all(inverse, "gx", split_axis=0, concat_axis=1, tiled=True)
    slabs = einsum("xzy,yk->xzk", slabs, table_y)
    returned = lax.all_to_all(slabs, "gy", split_axis=2, concat_axis=1, tiled=True)
    block = einsum("xzy,zk->xyk", returned, table_z)

    low = lax.ppermute(block[cells_x - LOW :], "gx", forward_x)
    high = lax.ppermute(block[:HIGH], "gx", backward_x)
    block = jnp.concatenate([low, block, high], 0)
    low = lax.ppermute(block[:, cells_y - LOW :], "gy", forward_y)
    high = lax.ppermute(block[:, :HIGH], "gy", backward_y)
    spare = jnp.zeros((wide_x, TILE - LOW - HIGH, depth), jnp.float32)
    field = jnp.concatenate([low, block, high, spare], 1)

    return pl.pallas_call(
        functools.partial(sample_kernel, rows_y),
        out_shape=jax.ShapeDtypeStruct((tile_count, point_count), jnp.float32),
        in_specs=[smem, smem] + [vmem] * 9,
        out_specs=vmem,
        compiler_params=params,
        cost_estimate=cost,
        name="sample",
    )(tile_grid, counts, values, noise, *places, field)


def solution(mesh):
    in_specs = (
        P(("gx", "gy"), None),
        P(("gx", "gy"), None),
        P(None, ("gx", "gy"), None),
        P(None, ("gx", "gy"), None),
        P(("gx", "gy"), None),
        P(("gx", "gy")),
        P(("gx", "gy")),
        P(),
        P(),
        P(),
    )
    out_specs = P(("gx", "gy"), None)
    return jax.shard_map(body, mesh=mesh, in_specs=in_specs, out_specs=out_specs, check_vma=False)
```

```python
import functools
import math

import jax
import jax.numpy as jnp
import numpy as np
from jax import lax
from jax.experimental import pallas as pl
from jax.experimental.pallas import tpu as pltpu
from jax.sharding import PartitionSpec as P

TILE = 8
SIDE = 11
WINDOW = 16
GROUP = 8
LOW = 1
HIGH = 2
VMEM_BYTES = 48 * 1024 * 1024


def ring(axis):
    count = lax.axis_size(axis)
    forward = [(i, (i + 1) % count) for i in range(count)]
    return forward, [(target, source) for source, target in forward]


def cubic_taps(fraction):
    square = fraction * fraction
    cubed = square * fraction
    return (
        -0.5 * cubed + square - 0.5 * fraction,
        1.5 * cubed - 2.5 * square + 1.0,
        -1.5 * cubed + 2.0 * square + 0.5 * fraction,
        0.5 * cubed - 0.5 * square,
    )


def cas_table(length):
    counter = np.arange(length, dtype=np.int64)
    radians = (counter[:, None] * counter[None, :] % length) * (2.0 * math.pi / length)
    return jnp.asarray((np.cos(radians) + np.sin(radians)).astype(np.float32))


def halves(array):
    top = array.astype(jnp.bfloat16)
    return top, (array - top.astype(jnp.float32)).astype(jnp.bfloat16)


def split_dot(left, right, dims):
    left_top, left_rest = halves(left)
    right_top, right_rest = halves(right)

    def dot(a, b):
        return lax.dot_general(a, b, (dims, ((), ())), preferred_element_type=jnp.float32)

    return dot(left_top, right_top) + (dot(left_top, right_rest) + dot(left_rest, right_top))


def box_weights(taps, start, row):
    delta = lax.broadcasted_iota(jnp.int32, (WINDOW, start.shape[1]), 0) - start[row : row + 1]
    weight = jnp.zeros(delta.shape, jnp.float32)
    for offset in range(4):
        weight = jnp.where(delta == offset, taps[offset][row : row + 1], weight)
    return weight


def column_weights(taps, start, row, depth):
    delta = lax.broadcasted_iota(jnp.int32, (depth, start.shape[1]), 0) - start[row : row + 1] + 1
    delta = jnp.where(delta < 0, delta + depth, delta)
    delta = jnp.where(delta >= depth, delta - depth, delta)
    weight = jnp.zeros(delta.shape, jnp.float32)
    for offset in range(4):
        weight = jnp.where(delta == offset, taps[offset][row : row + 1], weight)
    return weight


def group_rows(refs, first):
    return [ref[pl.ds(first, GROUP), :] for ref in refs]


def spread_kernel(
    rows_y, tile_grid, counts, values, fx, fy, fz, cx, cy, cz, padded
):
    depth = padded.shape[2]
    points = values.shape[1]
    padded[...] = jnp.zeros_like(padded)

    def step(index, carry):
        first = pl.multiple_of(index * GROUP, GROUP)
        value, f0, f1, f2, c0, c1, c2 = group_rows((values, fx, fy, fz, cx, cy, cz), first)
        taps_x, taps_y, taps_z = cubic_taps(f0), cubic_taps(f1), cubic_taps(f2)
        slot = lax.broadcasted_iota(jnp.int32, (1, points), 1)
        boxes = []
        for row in range(GROUP):
            source = jnp.where(slot < counts[first + row], value[row : row + 1], 0.0)
            wide_x = box_weights(taps_x, c0, row)
            wide_y = box_weights(taps_y, c1, row) * source
            plane = jnp.concatenate([wide_y[y : y + 1] * wide_x for y in range(SIDE)], 0)
            column = column_weights(taps_z, c2, row, depth)
            boxes.append(split_dot(plane, column, ((1,), (1,))))
        for row in range(GROUP):
            owner = tile_grid[first + row]
            at_x = pl.multiple_of((owner // rows_y) * TILE, TILE)
            at_y = lax.rem(owner, rows_y) * TILE
            padded[pl.ds(at_y, SIDE), pl.ds(at_x, WINDOW), :] += boxes[row].reshape(
                SIDE, WINDOW, depth
            )
        return carry

    lax.fori_loop(0, values.shape[0] // GROUP, step, 0)


def sample_kernel(
    rows_y, tile_grid, counts, values, noise, fx, fy, fz, cx, cy, cz, field, product
):
    depth = field.shape[2]
    points = values.shape[1]

    def step(index, carry):
        first = pl.multiple_of(index * GROUP, GROUP)
        value, level, f0, f1, f2, c0, c1, c2 = group_rows(
            (values, noise, fx, fy, fz, cx, cy, cz), first
        )
        taps_x, taps_y, taps_z = cubic_taps(f0), cubic_taps(f1), cubic_taps(f2)
        slot = lax.broadcasted_iota(jnp.int32, (1, points), 1)
        rows = []
        for row in range(GROUP):
            owner = tile_grid[first + row]
            at_x = pl.multiple_of((owner // rows_y) * TILE, TILE)
            at_y = lax.rem(owner, rows_y) * TILE
            box = field[pl.ds(at_y, SIDE), pl.ds(at_x, WINDOW), :].reshape(SIDE * WINDOW, depth)
            column = column_weights(taps_z, c2, row, depth)
            along = split_dot(box, column, ((1,), (0,))).reshape(SIDE, WINDOW, points)
            wide_x = box_weights(taps_x, c0, row)
            wide_y = box_weights(taps_y, c1, row)
            total = along[0] * wide_y[0:1]
            for y in range(1, SIDE):
                total = total + along[y] * wide_y[y : y + 1]
            sampled = jnp.sum(total * wide_x, axis=0, keepdims=True)
            result = level[row : row + 1] * value[row : row + 1] + sampled
            rows.append(jnp.where(slot < counts[first + row], result, 0.0))
        product[pl.ds(first, GROUP), :] = jnp.concatenate(rows, 0)
        return carry

    lax.fori_loop(0, values.shape[0] // GROUP, step, 0)


def remote(source, target, send, recv, axis, peer):
    return pltpu.make_async_remote_copy(
        src_ref=source,
        dst_ref=target,
        send_sem=send,
        recv_sem=recv,
        device_id={axis: peer},
        device_id_type=pl.DeviceIdType.MESH,
    )


def planes_kernel(
    ranks_x,
    ranks_y,
    chunks,
    scale,
    rate_z,
    rate_x,
    rate_y,
    x_top,
    x_rest,
    y_top,
    y_rest,
    turned,
    returned,
    pencils,
    outgoing,
    planes,
    slabs,
    y_send,
    y_recv,
    x_send,
    x_recv,
    back_x_send,
    back_x_recv,
    back_y_send,
    back_y_recv,
    local,
):
    me_x, me_y = lax.axis_index("gx"), lax.axis_index("gy")
    group = planes.shape[2]
    cells_x = planes.shape[4]
    cells_y = turned.shape[1]
    per_chunk = ranks_x * group
    per_rank = chunks * per_chunk
    peers_x = [lax.rem(me_x + step, ranks_x) for step in range(1, ranks_x)]
    peers_y = [lax.rem(me_y + step, ranks_y) for step in range(1, ranks_y)]

    barrier = pltpu.get_barrier_semaphore()
    for axis, peers in (("gx", peers_x), ("gy", peers_y)):
        for peer in peers:
            pl.semaphore_signal(
                barrier, inc=1, device_id={axis: peer}, device_id_type=pl.DeviceIdType.MESH
            )
    pl.semaphore_wait(barrier, ranks_x + ranks_y - 2)

    def planes_of(ref, rank, chunk):
        return ref.at[pl.ds(rank * per_rank + chunk * per_chunk, per_chunk)]

    def rows_of(chunk, rank):
        return pencils.at[chunk, :, pl.ds(pl.multiple_of(rank * cells_y, cells_y), cells_y)]

    def forward_y(chunk, peer):
        return remote(
            planes_of(turned, peer, chunk), rows_of(chunk, me_y),
            y_send.at[chunk, peer], y_recv.at[chunk, me_y], "gy", peer,
        )

    def arrived_y(chunk, peer):
        return remote(
            planes_of(turned, peer, chunk), rows_of(chunk, peer),
            y_send.at[chunk, peer], y_recv.at[chunk, peer], "gy", peer,
        )

    def own_y(chunk):
        return pltpu.make_async_copy(
            planes_of(turned, me_y, chunk), rows_of(chunk, me_y), local.at[0, chunk]
        )

    def forward_x(chunk, peer, slot):
        return remote(
            outgoing.at[chunk, peer], planes.at[chunk, slot],
            x_send.at[chunk, peer], x_recv.at[chunk, slot], "gx", peer,
        )

    def own_x(chunk):
        return pltpu.make_async_copy(
            outgoing.at[chunk, me_x], planes.at[chunk, me_x], local.at[1, chunk]
        )

    def back_x(chunk, peer, slot):
        return remote(
            planes.at[chunk, peer], slabs.at[chunk, slot],
            back_x_send.at[chunk, peer], back_x_recv.at[chunk, slot], "gx", peer,
        )

    def own_back_x(chunk):
        return pltpu.make_async_copy(
            planes.at[chunk, me_x], slabs.at[chunk, me_x], local.at[2, chunk]
        )

    def back_y(chunk, peer, slot):
        return remote(
            rows_of(chunk, peer), planes_of(returned, slot, chunk),
            back_y_send.at[chunk, peer], back_y_recv.at[chunk, slot], "gy", peer,
        )

    def own_back_y(chunk):
        return pltpu.make_async_copy(
            rows_of(chunk, me_y), planes_of(returned, me_y, chunk), local.at[3, chunk]
        )

    def table_dot(top, rest, right):
        right_top, right_rest = halves(right)

        def dot(a, b):
            return jnp.dot(a, b, preferred_element_type=jnp.float32)

        return dot(top, right_top) + (dot(top, right_rest) + dot(rest, right_top))

    def dot_table(left, top, rest):
        left_top, left_rest = halves(left)

        def dot(a, b):
            return jnp.dot(a, b, preferred_element_type=jnp.float32)

        return dot(left_top, top) + (dot(left_top, rest) + dot(left_rest, top))

    def send(chunk):
        own_y(chunk).start()
        for peer in peers_y:
            forward_y(chunk, peer).start()

    def along_y(chunk):
        own_y(chunk).wait()
        for peer in peers_y:
            arrived_y(chunk, peer).wait_recv()

        def one(index, carry):
            owner, plane = index // group, lax.rem(index, group)
            outgoing[chunk, owner, plane] = table_dot(
                y_top[...], y_rest[...], pencils[chunk, index]
            )
            return carry

        lax.fori_loop(0, per_chunk, one, 0)
        own_x(chunk).start()
        for peer in peers_x:
            forward_x(chunk, peer, me_x).start()

    def along_x(chunk):
        own_x(chunk).wait()
        for peer in peers_x:
            forward_x(chunk, peer, peer).wait_recv()

        def one(plane, carry):
            whole = jnp.concatenate(
                [planes[chunk, rank, plane] for rank in range(ranks_x)], 1
            )
            coeffs = dot_table(whole, x_top[...], x_rest[...])
            at_z = me_y * per_rank + chunk * per_chunk + me_x * group + plane
            denom = 1.0 + rate_x[...] + rate_y[...] + rate_z[at_z]
            weighted = coeffs * (scale / (denom * denom))
            inverse = dot_table(weighted, x_top[...], x_rest[...])
            for rank in range(ranks_x):
                planes[chunk, rank, plane] = inverse[:, rank * cells_x : (rank + 1) * cells_x]
            return carry

        lax.fori_loop(0, group, one, 0)
        own_back_x(chunk).start()
        for peer in peers_x:
            back_x(chunk, peer, me_x).start()

    def back_along_y(chunk):
        own_back_x(chunk).wait()
        for peer in peers_x:
            back_x(chunk, peer, peer).wait_recv()

        def one(index, carry):
            owner, plane = index // group, lax.rem(index, group)
            pencils[chunk, index] = table_dot(y_top[...], y_rest[...], slabs[chunk, owner, plane])
            return carry

        lax.fori_loop(0, per_chunk, one, 0)
        own_back_y(chunk).start()
        for peer in peers_y:
            back_y(chunk, peer, me_y).start()

    ahead = min(2, chunks)
    for chunk in range(ahead):
        send(chunk)

    def step(index, carry):
        @pl.when(index < chunks)
        def _():
            along_y(index)
            for peer in peers_y:
                forward_y(index, peer).wait_send()

        @pl.when(index + ahead < chunks)
        def _():
            send(index + ahead)

        @pl.when((index >= 1) & (index <= chunks))
        def _():
            along_x(index - 1)

        @pl.when(index >= 2)
        def _():
            back_along_y(index - 2)

        return carry

    lax.fori_loop(0, chunks + 2, step, 0)

    def finish(chunk, carry):
        own_back_y(chunk).wait()
        for peer in peers_x:
            forward_x(chunk, peer, me_x).wait_send()
            back_x(chunk, peer, me_x).wait_send()
        for peer in peers_y:
            back_y(chunk, peer, me_y).wait_send()
            back_y(chunk, peer, peer).wait_recv()
        return carry

    lax.fori_loop(0, chunks, finish, 0)


def smooth_planes(turned, rate_x, rate_y, rate_z, ranks_x, ranks_y):
    depth, cells_y, cells_x = turned.shape
    full_x, full_y = rate_x.shape[0], rate_y.shape[0]
    planes_dev = depth // (ranks_x * ranks_y)
    chunks = math.gcd(planes_dev, 4)
    group = planes_dev // chunks
    x_top, x_rest = halves(cas_table(full_x))
    y_top, y_rest = halves(cas_table(full_y))
    vmem = pl.BlockSpec(memory_space=pltpu.VMEM)
    anywhere = pl.BlockSpec(memory_space=pl.ANY)
    block = (chunks, ranks_x, group, full_y, cells_x)
    sems_x = pltpu.SemaphoreType.DMA((chunks, ranks_x))
    sems_y = pltpu.SemaphoreType.DMA((chunks, ranks_y))
    flops = 6 * 2 * turned.size * (full_x + full_y) * 2
    return pl.pallas_call(
        functools.partial(
            planes_kernel, ranks_x, ranks_y, chunks, 4.0 / (full_x * full_y * depth)
        ),
        out_shape=jax.ShapeDtypeStruct(turned.shape, jnp.float32),
        in_specs=[pl.BlockSpec(memory_space=pltpu.SMEM)] + [vmem] * 6 + [anywhere],
        out_specs=anywhere,
        scratch_shapes=[
            pltpu.VMEM((chunks, ranks_x * group, full_y, cells_x), jnp.float32),
            pltpu.VMEM(block, jnp.float32),
            pltpu.VMEM(block, jnp.float32),
            pltpu.VMEM(block, jnp.float32),
            sems_y, sems_y, sems_x, sems_x, sems_x, sems_x, sems_y, sems_y,
            pltpu.SemaphoreType.DMA((4, chunks)),
        ],
        compiler_params=pltpu.CompilerParams(
            collective_id=0, has_side_effects=True, vmem_limit_bytes=VMEM_BYTES
        ),
        cost_estimate=pl.CostEstimate(
            flops=flops, bytes_accessed=8 * turned.size, transcendentals=0
        ),
        name="smooth",
    )(
        rate_z, rate_x[None, :], rate_y[:, None], x_top, x_rest, y_top, y_rest, turned
    )


def body(values, noise, fractions, cell_xy, cell_z, tile_grid, counts, rate_x, rate_y, rate_z):
    tile_count, point_count = values.shape
    ranks_x = lax.axis_size("gx")
    ranks_y = lax.axis_size("gy")
    full_x = rate_x.shape[0]
    full_y = rate_y.shape[0]
    depth = rate_z.shape[0]
    cells_x = full_x // ranks_x
    cells_y = full_y // ranks_y
    rows_y = cells_y // TILE
    wide_x = cells_x + TILE
    wide_y = cells_y + LOW + HIGH
    smem = pl.BlockSpec(memory_space=pltpu.SMEM)
    vmem = pl.BlockSpec(memory_space=pltpu.VMEM)
    params = pltpu.CompilerParams(vmem_limit_bytes=VMEM_BYTES)
    places = (
        fractions[0], fractions[1], fractions[2], cell_xy[0], cell_xy[1], cell_z,
    )
    flops = 6 * tile_count * SIDE * WINDOW * point_count * depth
    cost = pl.CostEstimate(
        flops=flops, bytes_accessed=4 * wide_x * wide_y * depth, transcendentals=0
    )
    padded = pl.pallas_call(
        functools.partial(spread_kernel, rows_y),
        out_shape=jax.ShapeDtypeStruct((wide_y, wide_x, depth), jnp.float32),
        in_specs=[smem, smem] + [vmem] * 7,
        out_specs=vmem,
        compiler_params=params,
        cost_estimate=cost,
        name="spread",
    )(tile_grid, counts, values, *places)

    forward_x, backward_x = ring("gx")
    forward_y, backward_y = ring("gy")
    from_low = lax.ppermute(padded[cells_y + LOW :], "gy", forward_y)
    from_high = lax.ppermute(padded[:LOW], "gy", backward_y)
    padded = jnp.concatenate(
        [
            padded[LOW : LOW + HIGH] + from_low,
            padded[LOW + HIGH : cells_y],
            padded[cells_y : cells_y + LOW] + from_high,
        ],
        0,
    )
    from_low = lax.ppermute(
        padded[:, cells_x + LOW : cells_x + LOW + HIGH], "gx", forward_x
    )
    from_high = lax.ppermute(padded[:, :LOW], "gx", backward_x)
    spread_grid = jnp.concatenate(
        [
            padded[:, LOW : LOW + HIGH] + from_low,
            padded[:, LOW + HIGH : cells_x],
            padded[:, cells_x : cells_x + LOW] + from_high,
        ],
        1,
    )

    table_z = cas_table(depth)
    einsum = functools.partial(jnp.einsum, precision=lax.Precision.HIGH)
    turned = einsum("kz,yxz->kyx", table_z, spread_grid)
    returned = smooth_planes(turned, rate_x, rate_y, rate_z, ranks_x, ranks_y)
    block = einsum("kyx,kz->yxz", returned, table_z)

    low = lax.ppermute(block[cells_y - LOW :], "gy", forward_y)
    high = lax.ppermute(block[:HIGH], "gy", backward_y)
    block = jnp.concatenate([low, block, high], 0)
    low = lax.ppermute(block[:, cells_x - LOW :], "gx", forward_x)
    high = lax.ppermute(block[:, :HIGH], "gx", backward_x)
    spare = jnp.zeros((wide_y, TILE - LOW - HIGH, depth), jnp.float32)
    field = jnp.concatenate([low, block, high, spare], 1)

    return pl.pallas_call(
        functools.partial(sample_kernel, rows_y),
        out_shape=jax.ShapeDtypeStruct((tile_count, point_count), jnp.float32),
        in_specs=[smem, smem] + [vmem] * 9,
        out_specs=vmem,
        compiler_params=params,
        cost_estimate=cost,
        name="sample",
    )(tile_grid, counts, values, noise, *places, field)


def solution(mesh):
    in_specs = (
        P(("gx", "gy"), None),
        P(("gx", "gy"), None),
        P(None, ("gx", "gy"), None),
        P(None, ("gx", "gy"), None),
        P(("gx", "gy"), None),
        P(("gx", "gy")),
        P(("gx", "gy")),
        P(),
        P(),
        P(),
    )
    out_specs = P(("gx", "gy"), None)
    return jax.shard_map(body, mesh=mesh, in_specs=in_specs, out_specs=out_specs, check_vma=False)
```

```python
import functools
import math

import jax
import jax.numpy as jnp
import numpy as np
from jax import lax
from jax.experimental import pallas as pl
from jax.experimental.pallas import tpu as pltpu
from jax.sharding import PartitionSpec as P

TILE = 8
SIDE = 11
WINDOW = 16
GROUP = 8
LOW = 1
HIGH = 2
VMEM_BYTES = 48 * 1024 * 1024


def ring(axis):
    count = lax.axis_size(axis)
    forward = [(i, (i + 1) % count) for i in range(count)]
    return forward, [(target, source) for source, target in forward]


def cubic_taps(fraction):
    square = fraction * fraction
    cubed = square * fraction
    return (
        -0.5 * cubed + square - 0.5 * fraction,
        1.5 * cubed - 2.5 * square + 1.0,
        -1.5 * cubed + 2.0 * square + 0.5 * fraction,
        0.5 * cubed - 0.5 * square,
    )


def cas_table(length):
    counter = np.arange(length, dtype=np.int64)
    radians = (counter[:, None] * counter[None, :] % length) * (2.0 * math.pi / length)
    return jnp.asarray((np.cos(radians) + np.sin(radians)).astype(np.float32))


def halves(array):
    top = array.astype(jnp.bfloat16)
    return top, (array - top.astype(jnp.float32)).astype(jnp.bfloat16)


def product_dot(left, right, dims):
    return lax.dot_general(left, right, (dims, ((), ())), preferred_element_type=jnp.float32)


def box_weights(taps, start, row):
    delta = lax.broadcasted_iota(jnp.int32, (WINDOW, start.shape[1]), 0) - start[row : row + 1]
    weight = jnp.zeros(delta.shape, jnp.float32)
    for offset in range(4):
        weight = jnp.where(delta == offset, taps[offset][row : row + 1], weight)
    return weight


PACK = 16


def column_positions(start, depth):
    positions = []
    for offset in range(4):
        position = start + (offset - 1)
        position = jnp.where(position < 0, position + depth, position)
        positions.append(jnp.where(position >= depth, position - depth, position))
    return positions


def packed_row(array, row, dtype):
    return jnp.broadcast_to(array[row : row + 1], (PACK, array.shape[1])).astype(dtype)


def column_weights(taps, positions, row, cells):
    top = jnp.zeros(cells.shape, jnp.bfloat16)
    rest = jnp.zeros(cells.shape, jnp.bfloat16)
    for offset in range(4):
        here = cells == packed_row(positions[offset], row, jnp.int16)[None]
        first = taps[offset].astype(jnp.bfloat16).astype(jnp.float32)
        top = jnp.where(here, packed_row(first, row, jnp.bfloat16)[None], top)
        second = taps[offset] - first
        rest = jnp.where(here, packed_row(second, row, jnp.bfloat16)[None], rest)
    flat = (cells.shape[0] * PACK, cells.shape[2])
    return top.reshape(flat), rest.reshape(flat)


def column_cells(depth, points):
    groups = depth // PACK
    shape = (groups, PACK, points)
    cells = lax.broadcasted_iota(jnp.int32, shape, 0) * PACK
    return (cells + lax.broadcasted_iota(jnp.int32, shape, 1)).astype(jnp.int16)


def group_rows(refs, first):
    return [ref[pl.ds(first, GROUP), :] for ref in refs]


def spread_kernel(
    rows_y, tile_grid, counts, values, fx, fy, fz, cx, cy, cz, padded
):
    depth = padded.shape[2]
    points = values.shape[1]
    padded[...] = jnp.zeros_like(padded)

    cells = column_cells(depth, points)

    def step(index, carry):
        first = pl.multiple_of(index * GROUP, GROUP)
        value, f0, f1, f2, c0, c1, c2 = group_rows((values, fx, fy, fz, cx, cy, cz), first)
        taps_x, taps_y, taps_z = cubic_taps(f0), cubic_taps(f1), cubic_taps(f2)
        positions = column_positions(c2, depth)
        slot = lax.broadcasted_iota(jnp.int32, (1, points), 1)
        boxes = []
        for row in range(GROUP):
            source = jnp.where(slot < counts[first + row], value[row : row + 1], 0.0)
            wide_x = box_weights(taps_x, c0, row)
            wide_y = box_weights(taps_y, c1, row) * source
            plane = jnp.concatenate([wide_y[y : y + 1] * wide_x for y in range(SIDE)], 0)
            top, rest = column_weights(taps_z, positions, row, cells)
            plane_top, plane_rest = halves(plane)
            boxes.append(
                product_dot(
                    jnp.concatenate([plane_top, plane_rest], 1),
                    jnp.concatenate([top, top], 1),
                    ((1,), (1,)),
                )
                + product_dot(plane_top, rest, ((1,), (1,)))
            )
        for row in range(GROUP):
            owner = tile_grid[first + row]
            at_x = pl.multiple_of((owner // rows_y) * TILE, TILE)
            at_y = lax.rem(owner, rows_y) * TILE
            padded[pl.ds(at_y, SIDE), pl.ds(at_x, WINDOW), :] += boxes[row].reshape(
                SIDE, WINDOW, depth
            )
        return carry

    lax.fori_loop(0, values.shape[0] // GROUP, step, 0)


def sample_kernel(
    rows_y, tile_grid, counts, values, noise, fx, fy, fz, cx, cy, cz, field, product
):
    depth = field.shape[2]
    points = values.shape[1]

    cells = column_cells(depth, points)

    def step(index, carry):
        first = pl.multiple_of(index * GROUP, GROUP)
        value, level, f0, f1, f2, c0, c1, c2 = group_rows(
            (values, noise, fx, fy, fz, cx, cy, cz), first
        )
        taps_x, taps_y, taps_z = cubic_taps(f0), cubic_taps(f1), cubic_taps(f2)
        positions = column_positions(c2, depth)
        slot = lax.broadcasted_iota(jnp.int32, (1, points), 1)
        rows = []
        for row in range(GROUP):
            owner = tile_grid[first + row]
            at_x = pl.multiple_of((owner // rows_y) * TILE, TILE)
            at_y = lax.rem(owner, rows_y) * TILE
            box = field[pl.ds(at_y, SIDE), pl.ds(at_x, WINDOW), :].reshape(SIDE * WINDOW, depth)
            top, rest = column_weights(taps_z, positions, row, cells)
            box_top, box_rest = halves(box)
            both = product_dot(box_top, jnp.concatenate([top, rest], 1), ((1,), (0,)))
            along = both[:, :points] + both[:, points:] + product_dot(box_rest, top, ((1,), (0,)))
            along = along.reshape(SIDE, WINDOW, points)
            wide_x = box_weights(taps_x, c0, row)
            wide_y = box_weights(taps_y, c1, row)
            total = along[0] * wide_y[0:1]
            for y in range(1, SIDE):
                total = total + along[y] * wide_y[y : y + 1]
            sampled = jnp.sum(total * wide_x, axis=0, keepdims=True)
            result = level[row : row + 1] * value[row : row + 1] + sampled
            rows.append(jnp.where(slot < counts[first + row], result, 0.0))
        product[pl.ds(first, GROUP), :] = jnp.concatenate(rows, 0)
        return carry

    lax.fori_loop(0, values.shape[0] // GROUP, step, 0)


def remote(source, target, send, recv, axis, peer):
    return pltpu.make_async_remote_copy(
        src_ref=source,
        dst_ref=target,
        send_sem=send,
        recv_sem=recv,
        device_id={axis: peer},
        device_id_type=pl.DeviceIdType.MESH,
    )


def planes_kernel(
    ranks_x,
    ranks_y,
    chunks,
    scale,
    rate_z,
    rate_x,
    rate_y,
    x_top,
    x_rest,
    y_top,
    y_rest,
    turned,
    returned,
    pencils,
    outgoing,
    planes,
    slabs,
    y_send,
    y_recv,
    x_send,
    x_recv,
    back_x_send,
    back_x_recv,
    back_y_send,
    back_y_recv,
    local,
):
    me_x, me_y = lax.axis_index("gx"), lax.axis_index("gy")
    group = planes.shape[2]
    cells_x = planes.shape[4]
    cells_y = turned.shape[1]
    per_chunk = ranks_x * group
    per_rank = chunks * per_chunk
    peers_x = [lax.rem(me_x + step, ranks_x) for step in range(1, ranks_x)]
    peers_y = [lax.rem(me_y + step, ranks_y) for step in range(1, ranks_y)]

    barrier = pltpu.get_barrier_semaphore()
    for axis, peers in (("gx", peers_x), ("gy", peers_y)):
        for peer in peers:
            pl.semaphore_signal(
                barrier, inc=1, device_id={axis: peer}, device_id_type=pl.DeviceIdType.MESH
            )
    pl.semaphore_wait(barrier, ranks_x + ranks_y - 2)

    def planes_of(ref, rank, chunk):
        return ref.at[pl.ds(rank * per_rank + chunk * per_chunk, per_chunk)]

    def rows_of(chunk, rank):
        return pencils.at[chunk, :, pl.ds(pl.multiple_of(rank * cells_y, cells_y), cells_y)]

    def forward_y(chunk, peer):
        return remote(
            planes_of(turned, peer, chunk), rows_of(chunk, me_y),
            y_send.at[chunk, peer], y_recv.at[chunk, me_y], "gy", peer,
        )

    def arrived_y(chunk, peer):
        return remote(
            planes_of(turned, peer, chunk), rows_of(chunk, peer),
            y_send.at[chunk, peer], y_recv.at[chunk, peer], "gy", peer,
        )

    def own_y(chunk):
        return pltpu.make_async_copy(
            planes_of(turned, me_y, chunk), rows_of(chunk, me_y), local.at[0, chunk]
        )

    def forward_x(chunk, peer, slot):
        return remote(
            outgoing.at[chunk, peer], planes.at[chunk, slot],
            x_send.at[chunk, peer], x_recv.at[chunk, slot], "gx", peer,
        )

    def own_x(chunk):
        return pltpu.make_async_copy(
            outgoing.at[chunk, me_x], planes.at[chunk, me_x], local.at[1, chunk]
        )

    def back_x(chunk, peer, slot):
        return remote(
            planes.at[chunk, peer], slabs.at[chunk, slot],
            back_x_send.at[chunk, peer], back_x_recv.at[chunk, slot], "gx", peer,
        )

    def own_back_x(chunk):
        return pltpu.make_async_copy(
            planes.at[chunk, me_x], slabs.at[chunk, me_x], local.at[2, chunk]
        )

    def back_y(chunk, peer, slot):
        return remote(
            rows_of(chunk, peer), planes_of(returned, slot, chunk),
            back_y_send.at[chunk, peer], back_y_recv.at[chunk, slot], "gy", peer,
        )

    def own_back_y(chunk):
        return pltpu.make_async_copy(
            rows_of(chunk, me_y), planes_of(returned, me_y, chunk), local.at[3, chunk]
        )

    def table_dot(top, rest, right):
        right_top, right_rest = halves(right)

        def dot(a, b):
            return jnp.dot(a, b, preferred_element_type=jnp.float32)

        return dot(top, right_top) + (dot(top, right_rest) + dot(rest, right_top))

    def dot_table(left, top, rest):
        left_top, left_rest = halves(left)

        def dot(a, b):
            return jnp.dot(a, b, preferred_element_type=jnp.float32)

        return dot(left_top, top) + (dot(left_top, rest) + dot(left_rest, top))

    def send(chunk):
        own_y(chunk).start()
        for peer in peers_y:
            forward_y(chunk, peer).start()

    def along_y(chunk):
        own_y(chunk).wait()
        for peer in peers_y:
            arrived_y(chunk, peer).wait_recv()

        def one(index, carry):
            owner, plane = index // group, lax.rem(index, group)
            outgoing[chunk, owner, plane] = table_dot(
                y_top[...], y_rest[...], pencils[chunk, index]
            )
            return carry

        lax.fori_loop(0, per_chunk, one, 0)
        own_x(chunk).start()
        for peer in peers_x:
            forward_x(chunk, peer, me_x).start()

    def along_x(chunk):
        own_x(chunk).wait()
        for peer in peers_x:
            forward_x(chunk, peer, peer).wait_recv()

        def one(plane, carry):
            whole = jnp.concatenate(
                [planes[chunk, rank, plane] for rank in range(ranks_x)], 1
            )
            coeffs = dot_table(whole, x_top[...], x_rest[...])
            at_z = me_y * per_rank + chunk * per_chunk + me_x * group + plane
            denom = 1.0 + rate_x[...] + rate_y[...] + rate_z[at_z]
            weighted = coeffs * (scale / (denom * denom))
            inverse = dot_table(weighted, x_top[...], x_rest[...])
            for rank in range(ranks_x):
                planes[chunk, rank, plane] = inverse[:, rank * cells_x : (rank + 1) * cells_x]
            return carry

        lax.fori_loop(0, group, one, 0)
        own_back_x(chunk).start()
        for peer in peers_x:
            back_x(chunk, peer, me_x).start()

    def back_along_y(chunk):
        own_back_x(chunk).wait()
        for peer in peers_x:
            back_x(chunk, peer, peer).wait_recv()

        def one(index, carry):
            owner, plane = index // group, lax.rem(index, group)
            pencils[chunk, index] = table_dot(y_top[...], y_rest[...], slabs[chunk, owner, plane])
            return carry

        lax.fori_loop(0, per_chunk, one, 0)
        own_back_y(chunk).start()
        for peer in peers_y:
            back_y(chunk, peer, me_y).start()

    ahead = min(2, chunks)
    for chunk in range(ahead):
        send(chunk)

    def step(index, carry):
        @pl.when(index < chunks)
        def _():
            along_y(index)
            for peer in peers_y:
                forward_y(index, peer).wait_send()

        @pl.when(index + ahead < chunks)
        def _():
            send(index + ahead)

        @pl.when((index >= 1) & (index <= chunks))
        def _():
            along_x(index - 1)

        @pl.when(index >= 2)
        def _():
            back_along_y(index - 2)

        return carry

    lax.fori_loop(0, chunks + 2, step, 0)

    def finish(chunk, carry):
        own_back_y(chunk).wait()
        for peer in peers_x:
            forward_x(chunk, peer, me_x).wait_send()
            back_x(chunk, peer, me_x).wait_send()
        for peer in peers_y:
            back_y(chunk, peer, me_y).wait_send()
            back_y(chunk, peer, peer).wait_recv()
        return carry

    lax.fori_loop(0, chunks, finish, 0)


def smooth_planes(turned, rate_x, rate_y, rate_z, ranks_x, ranks_y):
    depth, cells_y, cells_x = turned.shape
    full_x, full_y = rate_x.shape[0], rate_y.shape[0]
    planes_dev = depth // (ranks_x * ranks_y)
    chunks = math.gcd(planes_dev, 4)
    group = planes_dev // chunks
    x_top, x_rest = halves(cas_table(full_x))
    y_top, y_rest = halves(cas_table(full_y))
    vmem = pl.BlockSpec(memory_space=pltpu.VMEM)
    anywhere = pl.BlockSpec(memory_space=pl.ANY)
    block = (chunks, ranks_x, group, full_y, cells_x)
    sems_x = pltpu.SemaphoreType.DMA((chunks, ranks_x))
    sems_y = pltpu.SemaphoreType.DMA((chunks, ranks_y))
    flops = 6 * 2 * turned.size * (full_x + full_y) * 2
    return pl.pallas_call(
        functools.partial(
            planes_kernel, ranks_x, ranks_y, chunks, 4.0 / (full_x * full_y * depth)
        ),
        out_shape=jax.ShapeDtypeStruct(turned.shape, jnp.float32),
        in_specs=[pl.BlockSpec(memory_space=pltpu.SMEM)] + [vmem] * 6 + [anywhere],
        out_specs=anywhere,
        scratch_shapes=[
            pltpu.VMEM((chunks, ranks_x * group, full_y, cells_x), jnp.float32),
            pltpu.VMEM(block, jnp.float32),
            pltpu.VMEM(block, jnp.float32),
            pltpu.VMEM(block, jnp.float32),
            sems_y, sems_y, sems_x, sems_x, sems_x, sems_x, sems_y, sems_y,
            pltpu.SemaphoreType.DMA((4, chunks)),
        ],
        compiler_params=pltpu.CompilerParams(
            collective_id=0, has_side_effects=True, vmem_limit_bytes=VMEM_BYTES
        ),
        cost_estimate=pl.CostEstimate(
            flops=flops, bytes_accessed=8 * turned.size, transcendentals=0
        ),
        name="smooth",
    )(
        rate_z, rate_x[None, :], rate_y[:, None], x_top, x_rest, y_top, y_rest, turned
    )


def body(values, noise, fractions, cell_xy, cell_z, tile_grid, counts, rate_x, rate_y, rate_z):
    tile_count, point_count = values.shape
    ranks_x = lax.axis_size("gx")
    ranks_y = lax.axis_size("gy")
    full_x = rate_x.shape[0]
    full_y = rate_y.shape[0]
    depth = rate_z.shape[0]
    cells_x = full_x // ranks_x
    cells_y = full_y // ranks_y
    rows_y = cells_y // TILE
    wide_x = cells_x + TILE
    wide_y = cells_y + LOW + HIGH
    smem = pl.BlockSpec(memory_space=pltpu.SMEM)
    vmem = pl.BlockSpec(memory_space=pltpu.VMEM)
    params = pltpu.CompilerParams(vmem_limit_bytes=VMEM_BYTES)
    places = (
        fractions[0], fractions[1], fractions[2], cell_xy[0], cell_xy[1], cell_z,
    )
    flops = 6 * tile_count * SIDE * WINDOW * point_count * depth
    cost = pl.CostEstimate(
        flops=flops, bytes_accessed=4 * wide_x * wide_y * depth, transcendentals=0
    )
    padded = pl.pallas_call(
        functools.partial(spread_kernel, rows_y),
        out_shape=jax.ShapeDtypeStruct((wide_y, wide_x, depth), jnp.float32),
        in_specs=[smem, smem] + [vmem] * 7,
        out_specs=vmem,
        compiler_params=params,
        cost_estimate=cost,
        name="spread",
    )(tile_grid, counts, values, *places)

    forward_x, backward_x = ring("gx")
    forward_y, backward_y = ring("gy")
    from_low = lax.ppermute(padded[cells_y + LOW :], "gy", forward_y)
    from_high = lax.ppermute(padded[:LOW], "gy", backward_y)
    padded = jnp.concatenate(
        [
            padded[LOW : LOW + HIGH] + from_low,
            padded[LOW + HIGH : cells_y],
            padded[cells_y : cells_y + LOW] + from_high,
        ],
        0,
    )
    from_low = lax.ppermute(
        padded[:, cells_x + LOW : cells_x + LOW + HIGH], "gx", forward_x
    )
    from_high = lax.ppermute(padded[:, :LOW], "gx", backward_x)
    spread_grid = jnp.concatenate(
        [
            padded[:, LOW : LOW + HIGH] + from_low,
            padded[:, LOW + HIGH : cells_x],
            padded[:, cells_x : cells_x + LOW] + from_high,
        ],
        1,
    )

    table_z = cas_table(depth)
    einsum = functools.partial(jnp.einsum, precision=lax.Precision.HIGH)
    turned = einsum("kz,yxz->kyx", table_z, spread_grid)
    returned = smooth_planes(turned, rate_x, rate_y, rate_z, ranks_x, ranks_y)
    block = einsum("kyx,kz->yxz", returned, table_z)

    low = lax.ppermute(block[cells_y - LOW :], "gy", forward_y)
    high = lax.ppermute(block[:HIGH], "gy", backward_y)
    block = jnp.concatenate([low, block, high], 0)
    low = lax.ppermute(block[:, cells_x - LOW :], "gx", forward_x)
    high = lax.ppermute(block[:, :HIGH], "gx", backward_x)
    spare = jnp.zeros((wide_y, TILE - LOW - HIGH, depth), jnp.float32)
    field = jnp.concatenate([low, block, high, spare], 1)

    return pl.pallas_call(
        functools.partial(sample_kernel, rows_y),
        out_shape=jax.ShapeDtypeStruct((tile_count, point_count), jnp.float32),
        in_specs=[smem, smem] + [vmem] * 9,
        out_specs=vmem,
        compiler_params=params,
        cost_estimate=cost,
        name="sample",
    )(tile_grid, counts, values, noise, *places, field)


def solution(mesh):
    in_specs = (
        P(("gx", "gy"), None),
        P(("gx", "gy"), None),
        P(None, ("gx", "gy"), None),
        P(None, ("gx", "gy"), None),
        P(("gx", "gy"), None),
        P(("gx", "gy")),
        P(("gx", "gy")),
        P(),
        P(),
        P(),
    )
    out_specs = P(("gx", "gy"), None)
    return jax.shard_map(body, mesh=mesh, in_specs=in_specs, out_specs=out_specs, check_vma=False)
```

```python
import functools
import math

import jax
import jax.numpy as jnp
import numpy as np
from jax import lax
from jax.experimental import pallas as pl
from jax.experimental.pallas import tpu as pltpu
from jax.sharding import PartitionSpec as P

TILE = 8
SIDE = 11
WINDOW = 16
GROUP = 8
LOW = 1
HIGH = 2
VMEM_BYTES = 48 * 1024 * 1024


def ring(axis):
    count = lax.axis_size(axis)
    forward = [(i, (i + 1) % count) for i in range(count)]
    return forward, [(target, source) for source, target in forward]


def cubic_taps(fraction):
    square = fraction * fraction
    cubed = square * fraction
    return (
        -0.5 * cubed + square - 0.5 * fraction,
        1.5 * cubed - 2.5 * square + 1.0,
        -1.5 * cubed + 2.0 * square + 0.5 * fraction,
        0.5 * cubed - 0.5 * square,
    )


def cas_table(length):
    counter = np.arange(length, dtype=np.int64)
    radians = (counter[:, None] * counter[None, :] % length) * (2.0 * math.pi / length)
    return jnp.asarray((np.cos(radians) + np.sin(radians)).astype(np.float32))


def halves(array):
    top = array.astype(jnp.bfloat16)
    return top, (array - top.astype(jnp.float32)).astype(jnp.bfloat16)


def product_dot(left, right, dims):
    return lax.dot_general(left, right, (dims, ((), ())), preferred_element_type=jnp.float32)


def box_weights(taps, start, row):
    delta = lax.broadcasted_iota(jnp.int32, (WINDOW, start.shape[1]), 0) - start[row : row + 1]
    weight = jnp.zeros(delta.shape, jnp.float32)
    for offset in range(4):
        weight = jnp.where(delta == offset, taps[offset][row : row + 1], weight)
    return weight


PACK = 16


def column_positions(start, depth):
    positions = []
    for offset in range(4):
        position = start + (offset - 1)
        position = jnp.where(position < 0, position + depth, position)
        positions.append(jnp.where(position >= depth, position - depth, position))
    return positions


def packed_row(array, row, dtype):
    return jnp.broadcast_to(array[row : row + 1], (PACK, array.shape[1])).astype(dtype)


def column_weights(taps, positions, row, cells):
    top = jnp.zeros(cells.shape, jnp.bfloat16)
    rest = jnp.zeros(cells.shape, jnp.bfloat16)
    for offset in range(4):
        here = cells == packed_row(positions[offset], row, jnp.int16)[None]
        first = taps[offset].astype(jnp.bfloat16).astype(jnp.float32)
        top = jnp.where(here, packed_row(first, row, jnp.bfloat16)[None], top)
        second = taps[offset] - first
        rest = jnp.where(here, packed_row(second, row, jnp.bfloat16)[None], rest)
    flat = (cells.shape[0] * PACK, cells.shape[2])
    return top.reshape(flat), rest.reshape(flat)


def column_cells(depth, points):
    groups = depth // PACK
    shape = (groups, PACK, points)
    cells = lax.broadcasted_iota(jnp.int32, shape, 0) * PACK
    return (cells + lax.broadcasted_iota(jnp.int32, shape, 1)).astype(jnp.int16)


def group_rows(refs, first):
    return [ref[pl.ds(first, GROUP), :] for ref in refs]


def spread_kernel(
    rows_y, tile_grid, counts, values, fx, fy, fz, cx, cy, cz,
    block, y_low, y_high, x_low, x_high, padded,
):
    depth = padded.shape[2]
    points = values.shape[1]
    padded[...] = jnp.zeros_like(padded)

    cells = column_cells(depth, points)

    def step(index, carry):
        first = pl.multiple_of(index * GROUP, GROUP)
        value, f0, f1, f2, c0, c1, c2 = group_rows((values, fx, fy, fz, cx, cy, cz), first)
        taps_x, taps_y, taps_z = cubic_taps(f0), cubic_taps(f1), cubic_taps(f2)
        positions = column_positions(c2, depth)
        slot = lax.broadcasted_iota(jnp.int32, (1, points), 1)
        boxes = []
        for row in range(GROUP):
            source = jnp.where(slot < counts[first + row], value[row : row + 1], 0.0)
            wide_x = box_weights(taps_x, c0, row)
            wide_y = box_weights(taps_y, c1, row) * source
            plane = jnp.concatenate([wide_y[y : y + 1] * wide_x for y in range(SIDE)], 0)
            top, rest = column_weights(taps_z, positions, row, cells)
            plane_top, plane_rest = halves(plane)
            boxes.append(
                product_dot(
                    jnp.concatenate([plane_top, plane_rest], 1),
                    jnp.concatenate([top, top], 1),
                    ((1,), (1,)),
                )
                + product_dot(plane_top, rest, ((1,), (1,)))
            )
        for row in range(GROUP):
            owner = tile_grid[first + row]
            at_x = pl.multiple_of((owner // rows_y) * TILE, TILE)
            at_y = lax.rem(owner, rows_y) * TILE
            padded[pl.ds(at_y, SIDE), pl.ds(at_x, WINDOW), :] += boxes[row].reshape(
                SIDE, WINDOW, depth
            )
        return carry

    lax.fori_loop(0, values.shape[0] // GROUP, step, 0)
    cells_y, cells_x = block.shape[0], block.shape[1]

    def move(row, carry):
        block[row] = padded[row + LOW, LOW : cells_x + LOW, :]
        x_low[row] = padded[row + LOW, :LOW, :]
        x_high[row] = padded[row + LOW, cells_x + LOW : cells_x + LOW + HIGH, :]
        return carry

    lax.fori_loop(0, cells_y, move, 0)
    y_low[...] = padded[:LOW]
    y_high[...] = padded[cells_y + LOW :]


def sample_kernel(
    rows_y, tile_grid, counts, values, noise, fx, fy, fz, cx, cy, cz,
    block, y_low, y_high, x_low, x_high, product, field,
):
    cells_y, cells_x = block.shape[0], block.shape[1]

    def move(row, carry):
        field[row + LOW, LOW : cells_x + LOW, :] = block[row]
        return carry

    lax.fori_loop(0, cells_y, move, 0)
    field[:LOW, LOW : cells_x + LOW, :] = y_low[...]
    field[cells_y + LOW :, LOW : cells_x + LOW, :] = y_high[...]

    def border(row, carry):
        field[row, :LOW, :] = x_low[row]
        field[row, cells_x + LOW : cells_x + LOW + HIGH, :] = x_high[row]
        field[row, cells_x + LOW + HIGH :, :] = jnp.zeros(
            (field.shape[1] - cells_x - LOW - HIGH, field.shape[2]), jnp.float32
        )
        return carry

    lax.fori_loop(0, field.shape[0], border, 0)
    depth = field.shape[2]
    points = values.shape[1]

    cells = column_cells(depth, points)

    def step(index, carry):
        first = pl.multiple_of(index * GROUP, GROUP)
        value, level, f0, f1, f2, c0, c1, c2 = group_rows(
            (values, noise, fx, fy, fz, cx, cy, cz), first
        )
        taps_x, taps_y, taps_z = cubic_taps(f0), cubic_taps(f1), cubic_taps(f2)
        positions = column_positions(c2, depth)
        slot = lax.broadcasted_iota(jnp.int32, (1, points), 1)
        rows = []
        for row in range(GROUP):
            owner = tile_grid[first + row]
            at_x = pl.multiple_of((owner // rows_y) * TILE, TILE)
            at_y = lax.rem(owner, rows_y) * TILE
            box = field[pl.ds(at_y, SIDE), pl.ds(at_x, WINDOW), :].reshape(SIDE * WINDOW, depth)
            top, rest = column_weights(taps_z, positions, row, cells)
            box_top, box_rest = halves(box)
            both = product_dot(box_top, jnp.concatenate([top, rest], 1), ((1,), (0,)))
            along = both[:, :points] + both[:, points:] + product_dot(box_rest, top, ((1,), (0,)))
            along = along.reshape(SIDE, WINDOW, points)
            wide_x = box_weights(taps_x, c0, row)
            wide_y = box_weights(taps_y, c1, row)
            total = along[0] * wide_y[0:1]
            for y in range(1, SIDE):
                total = total + along[y] * wide_y[y : y + 1]
            sampled = jnp.sum(total * wide_x, axis=0, keepdims=True)
            result = level[row : row + 1] * value[row : row + 1] + sampled
            rows.append(jnp.where(slot < counts[first + row], result, 0.0))
        product[pl.ds(first, GROUP), :] = jnp.concatenate(rows, 0)
        return carry

    lax.fori_loop(0, values.shape[0] // GROUP, step, 0)


def remote(source, target, send, recv, axis, peer):
    return pltpu.make_async_remote_copy(
        src_ref=source,
        dst_ref=target,
        send_sem=send,
        recv_sem=recv,
        device_id={axis: peer},
        device_id_type=pl.DeviceIdType.MESH,
    )


def planes_kernel(
    ranks_x,
    ranks_y,
    chunks,
    scale,
    rate_z,
    rate_x,
    rate_y,
    x_top,
    x_rest,
    y_top,
    y_rest,
    turned,
    returned,
    pencils,
    outgoing,
    planes,
    slabs,
    y_send,
    y_recv,
    x_send,
    x_recv,
    back_x_send,
    back_x_recv,
    back_y_send,
    back_y_recv,
    local,
):
    me_x, me_y = lax.axis_index("gx"), lax.axis_index("gy")
    group = planes.shape[2]
    cells_x = planes.shape[4]
    cells_y = turned.shape[1]
    per_chunk = ranks_x * group
    per_rank = chunks * per_chunk
    peers_x = [lax.rem(me_x + step, ranks_x) for step in range(1, ranks_x)]
    peers_y = [lax.rem(me_y + step, ranks_y) for step in range(1, ranks_y)]

    barrier = pltpu.get_barrier_semaphore()
    for axis, peers in (("gx", peers_x), ("gy", peers_y)):
        for peer in peers:
            pl.semaphore_signal(
                barrier, inc=1, device_id={axis: peer}, device_id_type=pl.DeviceIdType.MESH
            )
    pl.semaphore_wait(barrier, ranks_x + ranks_y - 2)

    def planes_of(ref, rank, chunk):
        return ref.at[pl.ds(rank * per_rank + chunk * per_chunk, per_chunk)]

    def rows_of(chunk, rank):
        return pencils.at[chunk, :, pl.ds(pl.multiple_of(rank * cells_y, cells_y), cells_y)]

    def forward_y(chunk, peer):
        return remote(
            planes_of(turned, peer, chunk), rows_of(chunk, me_y),
            y_send.at[chunk, peer], y_recv.at[chunk, me_y], "gy", peer,
        )

    def arrived_y(chunk, peer):
        return remote(
            planes_of(turned, peer, chunk), rows_of(chunk, peer),
            y_send.at[chunk, peer], y_recv.at[chunk, peer], "gy", peer,
        )

    def own_y(chunk):
        return pltpu.make_async_copy(
            planes_of(turned, me_y, chunk), rows_of(chunk, me_y), local.at[0, chunk]
        )

    def forward_x(chunk, peer, slot):
        return remote(
            outgoing.at[chunk, peer], planes.at[chunk, slot],
            x_send.at[chunk, peer], x_recv.at[chunk, slot], "gx", peer,
        )

    def own_x(chunk):
        return pltpu.make_async_copy(
            outgoing.at[chunk, me_x], planes.at[chunk, me_x], local.at[1, chunk]
        )

    def back_x(chunk, peer, slot):
        return remote(
            planes.at[chunk, peer], slabs.at[chunk, slot],
            back_x_send.at[chunk, peer], back_x_recv.at[chunk, slot], "gx", peer,
        )

    def own_back_x(chunk):
        return pltpu.make_async_copy(
            planes.at[chunk, me_x], slabs.at[chunk, me_x], local.at[2, chunk]
        )

    def back_y(chunk, peer, slot):
        return remote(
            rows_of(chunk, peer), planes_of(returned, slot, chunk),
            back_y_send.at[chunk, peer], back_y_recv.at[chunk, slot], "gy", peer,
        )

    def own_back_y(chunk):
        return pltpu.make_async_copy(
            rows_of(chunk, me_y), planes_of(returned, me_y, chunk), local.at[3, chunk]
        )

    def table_dot(top, rest, right):
        right_top, right_rest = halves(right)

        def dot(a, b):
            return jnp.dot(a, b, preferred_element_type=jnp.float32)

        return dot(top, right_top) + (dot(top, right_rest) + dot(rest, right_top))

    def dot_table(left, top, rest):
        left_top, left_rest = halves(left)

        def dot(a, b):
            return jnp.dot(a, b, preferred_element_type=jnp.float32)

        return dot(left_top, top) + (dot(left_top, rest) + dot(left_rest, top))

    def send(chunk):
        own_y(chunk).start()
        for peer in peers_y:
            forward_y(chunk, peer).start()

    def along_y(chunk):
        own_y(chunk).wait()
        for peer in peers_y:
            arrived_y(chunk, peer).wait_recv()

        def one(index, carry):
            owner, plane = index // group, lax.rem(index, group)
            outgoing[chunk, owner, plane] = table_dot(
                y_top[...], y_rest[...], pencils[chunk, index]
            )
            return carry

        lax.fori_loop(0, per_chunk, one, 0)
        own_x(chunk).start()
        for peer in peers_x:
            forward_x(chunk, peer, me_x).start()

    def along_x(chunk):
        own_x(chunk).wait()
        for peer in peers_x:
            forward_x(chunk, peer, peer).wait_recv()

        def one(plane, carry):
            whole = jnp.concatenate(
                [planes[chunk, rank, plane] for rank in range(ranks_x)], 1
            )
            coeffs = dot_table(whole, x_top[...], x_rest[...])
            at_z = me_y * per_rank + chunk * per_chunk + me_x * group + plane
            denom = 1.0 + rate_x[...] + rate_y[...] + rate_z[at_z]
            weighted = coeffs * (scale / (denom * denom))
            inverse = dot_table(weighted, x_top[...], x_rest[...])
            for rank in range(ranks_x):
                planes[chunk, rank, plane] = inverse[:, rank * cells_x : (rank + 1) * cells_x]
            return carry

        lax.fori_loop(0, group, one, 0)
        own_back_x(chunk).start()
        for peer in peers_x:
            back_x(chunk, peer, me_x).start()

    def back_along_y(chunk):
        own_back_x(chunk).wait()
        for peer in peers_x:
            back_x(chunk, peer, peer).wait_recv()

        def one(index, carry):
            owner, plane = index // group, lax.rem(index, group)
            pencils[chunk, index] = table_dot(y_top[...], y_rest[...], slabs[chunk, owner, plane])
            return carry

        lax.fori_loop(0, per_chunk, one, 0)
        own_back_y(chunk).start()
        for peer in peers_y:
            back_y(chunk, peer, me_y).start()

    ahead = min(2, chunks)
    for chunk in range(ahead):
        send(chunk)

    def step(index, carry):
        @pl.when(index < chunks)
        def _():
            along_y(index)
            for peer in peers_y:
                forward_y(index, peer).wait_send()

        @pl.when(index + ahead < chunks)
        def _():
            send(index + ahead)

        @pl.when((index >= 1) & (index <= chunks))
        def _():
            along_x(index - 1)

        @pl.when(index >= 2)
        def _():
            back_along_y(index - 2)

        return carry

    lax.fori_loop(0, chunks + 2, step, 0)

    def finish(chunk, carry):
        own_back_y(chunk).wait()
        for peer in peers_x:
            forward_x(chunk, peer, me_x).wait_send()
            back_x(chunk, peer, me_x).wait_send()
        for peer in peers_y:
            back_y(chunk, peer, me_y).wait_send()
            back_y(chunk, peer, peer).wait_recv()
        return carry

    lax.fori_loop(0, chunks, finish, 0)


def smooth_planes(turned, rate_x, rate_y, rate_z, ranks_x, ranks_y):
    depth, cells_y, cells_x = turned.shape
    full_x, full_y = rate_x.shape[0], rate_y.shape[0]
    planes_dev = depth // (ranks_x * ranks_y)
    chunks = math.gcd(planes_dev, 4)
    group = planes_dev // chunks
    x_top, x_rest = halves(cas_table(full_x))
    y_top, y_rest = halves(cas_table(full_y))
    vmem = pl.BlockSpec(memory_space=pltpu.VMEM)
    anywhere = pl.BlockSpec(memory_space=pl.ANY)
    block = (chunks, ranks_x, group, full_y, cells_x)
    sems_x = pltpu.SemaphoreType.DMA((chunks, ranks_x))
    sems_y = pltpu.SemaphoreType.DMA((chunks, ranks_y))
    flops = 6 * 2 * turned.size * (full_x + full_y) * 2
    return pl.pallas_call(
        functools.partial(
            planes_kernel, ranks_x, ranks_y, chunks, 4.0 / (full_x * full_y * depth)
        ),
        out_shape=jax.ShapeDtypeStruct(turned.shape, jnp.float32),
        in_specs=[pl.BlockSpec(memory_space=pltpu.SMEM)] + [vmem] * 6 + [anywhere],
        out_specs=anywhere,
        scratch_shapes=[
            pltpu.VMEM((chunks, ranks_x * group, full_y, cells_x), jnp.float32),
            pltpu.VMEM(block, jnp.float32),
            pltpu.VMEM(block, jnp.float32),
            pltpu.VMEM(block, jnp.float32),
            sems_y, sems_y, sems_x, sems_x, sems_x, sems_x, sems_y, sems_y,
            pltpu.SemaphoreType.DMA((4, chunks)),
        ],
        compiler_params=pltpu.CompilerParams(
            collective_id=0, has_side_effects=True, vmem_limit_bytes=VMEM_BYTES
        ),
        cost_estimate=pl.CostEstimate(
            flops=flops, bytes_accessed=8 * turned.size, transcendentals=0
        ),
        name="smooth",
    )(
        rate_z, rate_x[None, :], rate_y[:, None], x_top, x_rest, y_top, y_rest, turned
    )


def body(values, noise, fractions, cell_xy, cell_z, tile_grid, counts, rate_x, rate_y, rate_z):
    tile_count, point_count = values.shape
    ranks_x = lax.axis_size("gx")
    ranks_y = lax.axis_size("gy")
    full_x = rate_x.shape[0]
    full_y = rate_y.shape[0]
    depth = rate_z.shape[0]
    cells_x = full_x // ranks_x
    cells_y = full_y // ranks_y
    rows_y = cells_y // TILE
    wide_x = cells_x + TILE
    wide_y = cells_y + LOW + HIGH
    smem = pl.BlockSpec(memory_space=pltpu.SMEM)
    vmem = pl.BlockSpec(memory_space=pltpu.VMEM)
    params = pltpu.CompilerParams(vmem_limit_bytes=VMEM_BYTES)
    places = (
        fractions[0], fractions[1], fractions[2], cell_xy[0], cell_xy[1], cell_z,
    )
    flops = 6 * tile_count * SIDE * WINDOW * point_count * depth
    cost = pl.CostEstimate(
        flops=flops, bytes_accessed=4 * wide_x * wide_y * depth, transcendentals=0
    )
    block, y_low, y_high, x_low, x_high = pl.pallas_call(
        functools.partial(spread_kernel, rows_y),
        out_shape=[
            jax.ShapeDtypeStruct(shape, jnp.float32)
            for shape in (
                (cells_y, cells_x, depth),
                (LOW, wide_x, depth),
                (HIGH, wide_x, depth),
                (cells_y, LOW, depth),
                (cells_y, HIGH, depth),
            )
        ],
        in_specs=[smem, smem] + [vmem] * 7,
        out_specs=[vmem] * 5,
        scratch_shapes=[pltpu.VMEM((wide_y, wide_x, depth), jnp.float32)],
        compiler_params=params,
        cost_estimate=cost,
        name="spread",
    )(tile_grid, counts, values, *places)

    forward_x, backward_x = ring("gx")
    forward_y, backward_y = ring("gy")
    from_low = lax.ppermute(y_high, "gy", forward_y)
    from_high = lax.ppermute(y_low, "gy", backward_y)

    def with_edges(part, first, last):
        part = part.at[:HIGH].add(from_low[:, first:last])
        return part.at[cells_y - LOW :].add(from_high[:, first:last])

    inner = cells_x + LOW
    block = with_edges(block, LOW, inner)
    x_low = with_edges(x_low, 0, LOW)
    x_high = with_edges(x_high, inner, inner + HIGH)
    from_low = lax.ppermute(x_high, "gx", forward_x)
    from_high = lax.ppermute(x_low, "gx", backward_x)
    spread_grid = block.at[:, :HIGH].add(from_low).at[:, cells_x - LOW :].add(from_high)

    table_z = cas_table(depth)
    einsum = functools.partial(jnp.einsum, precision=lax.Precision.HIGH)
    turned = einsum("kz,yxz->kyx", table_z, spread_grid)
    returned = smooth_planes(turned, rate_x, rate_y, rate_z, ranks_x, ranks_y)
    block = einsum("kyx,kz->yxz", returned, table_z)

    y_low = lax.ppermute(block[cells_y - LOW :], "gy", forward_y)
    y_high = lax.ppermute(block[:HIGH], "gy", backward_y)

    def column(first, last):
        return jnp.concatenate([part[:, first:last] for part in (y_low, block, y_high)], 0)

    x_low = lax.ppermute(column(cells_x - LOW, cells_x), "gx", forward_x)
    x_high = lax.ppermute(column(0, HIGH), "gx", backward_x)

    return pl.pallas_call(
        functools.partial(sample_kernel, rows_y),
        out_shape=jax.ShapeDtypeStruct((tile_count, point_count), jnp.float32),
        in_specs=[smem, smem] + [vmem] * 13,
        out_specs=vmem,
        scratch_shapes=[pltpu.VMEM((wide_y, wide_x, depth), jnp.float32)],
        compiler_params=params,
        cost_estimate=cost,
        name="sample",
    )(
        tile_grid, counts, values, noise, *places, block, y_low, y_high, x_low, x_high
    )


def solution(mesh):
    in_specs = (
        P(("gx", "gy"), None),
        P(("gx", "gy"), None),
        P(None, ("gx", "gy"), None),
        P(None, ("gx", "gy"), None),
        P(("gx", "gy"), None),
        P(("gx", "gy")),
        P(("gx", "gy")),
        P(),
        P(),
        P(),
    )
    out_specs = P(("gx", "gy"), None)
    return jax.shard_map(body, mesh=mesh, in_specs=in_specs, out_specs=out_specs, check_vma=False)
```
